32 devices in a mesh: groups: 2 (over x), cache: 16 (over z, y, core).
Axes of the slice: x: 2, y: 2, z: 4, core: 2. Of those that a mesh axis runs over, the one named last changes fastest.
Arguments:
- page_store: bfloat16 [8192, 8, 1024], P(('groups', 'cache')), parts along dimension 0, may hold values from -6 to 6
- page_table: int32 [32, 256], P(('groups', 'cache')), parts along dimension 0, may hold values from 0 to 255, each once within a row
- recomp_pos: int32 [32, 128], P(('groups', 'cache')), parts along dimension 0, may hold values from 0 to 2047, as said below
- queries: bfloat16 [32, 128, 4096], P(('groups', 'cache')), parts along dimension 0, may hold values from -135 to 135
- fresh_kv: bfloat16 [32, 128, 1024], P(('groups', 'cache')), parts along dimension 0, may hold values from -5 to 5
Outputs:
- new_store: bfloat16 [8192, 8, 1024], P(('groups', 'cache')), parts along dimension 0
- attended: bfloat16 [32, 128, 4096], P(('groups', 'cache')), parts along dimension 0
The draws below stay inside these ranges and needn't reach their ends.
There are 2 independent parts, one for each index of `groups`. The reference program is written for one: setup_inputs(seed, part) draws one part's arguments, and reference() takes and returns one part's arrays. A program takes and returns all parts, laid end to end along the dimension named above; each array names one. Nothing has to cross between parts.
Inputs may be any that keep to these rules, and one draw needn't show every extreme that they name: `recomp_pos`: for each request the positions rise strictly, no two lie in one page of 8 tokens, and all lie in the first c * 512 tokens, where c, from 2 to 4, is the request's number of spans; some request joins 4 spans.
All inputs are finite; a program needn't handle non-finite values.
Results may differ from the reference program's by a relative error of at most 0.0039.
Values may be sent and summed in bfloat16 or wider, within the bound.
A program may use at most 64 MiB of HBM per device.

```python
import math
import jax
import jax.numpy as jnp
from jax import lax

HQ = 32
KVH = 4
HD = 128
SPAN = 512
PAGE = 8
MAXCH = 4
RECOMP = 128
REQS = 16
MAXPAGES = 256
KV_ROW = 1024
N_CACHE = 16


def shared_keys(key):
    base_keys = jnp.clip(jax.random.normal(jax.random.fold_in(key, 11), (REQS, RECOMP, KVH * HD), jnp.float32), -4.5, 4.5)
    picked_rows = jax.random.randint(jax.random.fold_in(key, 13), (REQS, 4), 1, RECOMP)
    strength = jax.random.uniform(jax.random.fold_in(key, 14), (REQS, 4), jnp.float32, 10.0, 30.0)
    row_ids = jnp.arange(RECOMP)
    matches = row_ids[None, None, :] == picked_rows[:, :, None]
    row_scale = jnp.max(jnp.where(matches, strength[:, :, None], 0.0), axis=1)
    key_part = base_keys
    return (key_part, row_scale)


def draw_fresh_kv(key, part):
    key_part, row_scale = shared_keys(key)
    key = jax.random.fold_in(key, 7)
    values = jnp.clip(jax.random.normal(key, (REQS, RECOMP, KVH * HD), jnp.float32), -4.5, 4.5)
    return jnp.concatenate([key_part, values], axis=-1).astype(jnp.bfloat16)


def draw_queries(key, part):
    key_part, row_scale = shared_keys(key)
    weight_on = 0.0
    key = jax.random.fold_in(key, 9)
    drawn = jnp.clip(jax.random.normal(key, (REQS, RECOMP, HQ, HD), jnp.float32), -4.5, 4.5)
    group_size = HQ // KVH
    rounded_keys = key_part.astype(jnp.bfloat16).astype(jnp.float32)
    aligned = jnp.repeat(rounded_keys.reshape(REQS, RECOMP, KVH, HD), group_size, axis=2) * row_scale[:, :, None, None]
    chosen = weight_on * row_scale > 0.0
    result = jnp.where(chosen[:, :, None, None], aligned, drawn)
    return result.reshape(REQS, RECOMP, HQ * HD).astype(jnp.bfloat16)


def draw_recomp_pos(key, part):
    key = jax.random.fold_in(key, 5)
    per_span = SPAN // PAGE
    span_totals = jax.random.randint(jax.random.fold_in(key, 1), (REQS,), 2, MAXCH + 1)
    longest = jax.random.randint(jax.random.fold_in(key, 2), (), 0, REQS)
    span_totals = jnp.where(jnp.arange(REQS) == longest, MAXCH, span_totals)
    live_pages = span_totals * per_span
    page_ids = jnp.arange(MAXPAGES, dtype=jnp.int32)
    ranking = jax.random.randint(jax.random.fold_in(key, 3), (REQS, MAXPAGES), 0, 2 ** 20) * MAXPAGES + page_ids[None, :]
    ranking = jnp.where(page_ids[None, :] < live_pages[:, None], ranking, 2 ** 30)
    chosen_pages = jnp.sort(jnp.argsort(ranking, axis=1, stable=True)[:, :RECOMP], axis=1)
    offsets = jax.random.randint(jax.random.fold_in(key, 4), (REQS, RECOMP), 0, PAGE)
    return (chosen_pages * PAGE + offsets).astype(jnp.int32)


def level_of(stream_key, dims, cuts, low, top_value):
    factor_of, own = 1.0, jax.random.fold_in(stream_key, 6)
    for position, shards_of in cuts:
        draws = jnp.exp(jax.random.uniform(jax.random.fold_in(own, position), (shards_of,), jnp.float32, low / len(cuts), top_value / len(cuts)))
        factor_of = factor_of * jnp.repeat(draws, dims[position] // shards_of).reshape([-1 if axis == position else 1 for axis in range(len(dims))])
    return factor_of


def scatter_about(own_key, shape, scale, bound, cuts=(), kind=jnp.bfloat16):
    drawn = scale * jax.random.normal(own_key, shape, jnp.float32)
    if cuts:
        drawn = drawn * level_of(own_key, shape, cuts, -0.22, 0.18)
    return jnp.clip(drawn, -bound, bound).astype(kind)


def setup_inputs(seed: int = 0, part: int = 0) -> dict:
    seeds = jax.random.split(jax.random.key(seed), 6)
    own_keys = jax.random.split(jax.random.fold_in(seeds[5], part), 6)
    page_store = scatter_about(own_keys[0], (N_CACHE * MAXPAGES, PAGE, KV_ROW), 1.0, 6.0, ((0, 16),))
    page_table = jax.vmap(lambda own: jax.random.permutation(own, MAXPAGES))(jax.random.split(own_keys[1], REQS)).reshape((REQS, MAXPAGES)).astype(jnp.int32)
    recomp_pos = draw_recomp_pos(jax.random.fold_in(jax.random.fold_in(seeds[5], part), 71), part)
    queries = draw_queries(jax.random.fold_in(jax.random.fold_in(seeds[5], part), 71), part)
    fresh_kv = draw_fresh_kv(jax.random.fold_in(jax.random.fold_in(seeds[5], part), 71), part)
    return dict(page_store=page_store, page_table=page_table, recomp_pos=recomp_pos, queries=queries, fresh_kv=fresh_kv)


def attention(query_rows, sequence, positions):
    row_count = query_rows.shape[0]
    group_size = HQ // KVH
    key_width = KVH * HD
    score_scale = 1.0 / math.sqrt(HD)
    q_heads = query_rows.astype(jnp.float32).reshape(row_count, KVH, group_size, HD)
    q_heads = q_heads.transpose(1, 2, 0, 3).reshape(KVH, group_size * row_count, HD)
    key_rows = sequence[:, :key_width].astype(jnp.float32).reshape(-1, KVH, HD)
    value_rows = sequence[:, key_width:].astype(jnp.float32).reshape(-1, KVH, HD)
    scores = jnp.einsum('gqd,kgd->gqk', q_heads, key_rows) * score_scale
    query_pos = jnp.tile(positions, group_size)
    key_pos = jnp.arange(sequence.shape[0], dtype=jnp.int32)
    scores = jnp.where(key_pos[None, None, :] <= query_pos[None, :, None], scores, -1e+30)
    row_max = lax.optimization_barrier(jnp.max(scores, axis=-1))
    weights = jnp.exp(scores - row_max[..., None])
    denominator = lax.optimization_barrier(jnp.sum(weights, axis=-1))
    probs = lax.optimization_barrier(weights.astype(jnp.bfloat16)).astype(jnp.float32)
    mixed = jnp.einsum('gqk,kgd->gqd', probs, value_rows) / denominator[..., None]
    mixed = mixed.reshape(KVH, group_size, row_count, HD).transpose(2, 0, 1, 3)
    return mixed.reshape(row_count, HQ * HD).astype(jnp.bfloat16)

def reference(page_store, page_table, recomp_pos, queries, fresh_kv):
    per_peer = MAXPAGES // N_CACHE
    page_index = recomp_pos // PAGE
    lane_index = recomp_pos % PAGE
    slot_pos = jnp.take_along_axis(page_table, page_index, axis=1)
    holder = slot_pos // per_peer
    owner_ids = jnp.arange(REQS, dtype=jnp.int32)[:, None]
    target = holder * MAXPAGES + owner_ids * per_peer + slot_pos % per_peer
    new_store = page_store.at[target.reshape(-1), lane_index.reshape(-1)].set(fresh_kv.reshape(-1, KV_ROW))
    grouped = page_store.reshape(N_CACHE, N_CACHE, per_peer, PAGE, KV_ROW)

    def one_request(owner):
        owned = jnp.take(grouped, owner, axis=1).reshape(MAXPAGES, PAGE, KV_ROW)
        order = jnp.take(page_table, owner, axis=0)
        sequence = owned[order].reshape(MAXPAGES * PAGE, KV_ROW)
        positions = jnp.take(recomp_pos, owner, axis=0)
        sequence = sequence.at[positions].set(jnp.take(fresh_kv, owner, axis=0))
        return attention(jnp.take(queries, owner, axis=0), sequence, positions)
    attended = lax.map(one_request, jnp.arange(REQS, dtype=jnp.int32))
    return (new_store, attended)
```

```python
import functools
import math

import jax
import jax.numpy as jnp
from jax import lax
from jax.experimental import pallas as pl
from jax.experimental.pallas import tpu as pltpu
from jax.sharding import PartitionSpec as P

HQ = 32
KVH = 4
HD = 128
GROUP = HQ // KVH
CHUNKS = 8
LANES = 128
MESH = pl.DeviceIdType.MESH
NEG = -1e30


def flip(index, bits):
    result = index
    weight = 1
    while weight <= bits:
        if bits & weight:
            own = lax.rem(lax.div(index, weight), 2)
            result = result + weight * (1 - 2 * own)
        weight *= 2
    return result


def chunk_order():
    half = CHUNKS // 2
    order = []
    for k in range(half):
        order += [k, half + k]
    return order


def kernel(
    n,
    table_col,
    pos_row,
    pos_col,
    store_hbm,
    queries_hbm,
    fresh_hbm,
    out_ref,
    rows_ref,
    kv,
    q_in,
    fresh,
    q_heads,
    key_pos,
    bias,
    row_max,
    row_sum,
    acc,
    payload,
    send_sem,
    recv_sem,
    pay_send_sem,
    pay_recv_sem,
    local_sem,
):
    me = lax.axis_index("cache")
    group = lax.axis_index("groups")
    tokens, width = kv.shape
    pages = table_col.shape[0]
    page_len = tokens // pages
    per_peer = pages // n
    piece = tokens // n
    chunk = tokens // CHUNKS
    peers_per_chunk = n // CHUNKS
    recomp = pos_row.shape[1]
    q_rows = GROUP * recomp
    scale = math.log2(math.e) / math.sqrt(HD)

    barrier = pltpu.get_barrier_semaphore()
    for d in range(1, n):
        pl.semaphore_signal(
            barrier, inc=1, device_id=(group, flip(me, d)), device_id_type=MESH
        )
    q_copy = pltpu.make_async_copy(queries_hbm, q_in, local_sem.at[0])
    fresh_copy = pltpu.make_async_copy(fresh_hbm, fresh, local_sem.at[1])
    own_rows = pl.ds(pl.multiple_of(me * piece, piece), piece)
    own_copy = pltpu.make_async_copy(store_hbm.at[own_rows], kv.at[own_rows], local_sem.at[2])
    fresh_copy.start()
    q_copy.start()
    own_copy.start()
    pl.semaphore_wait(barrier, n - 1)

    def piece_copy(d):
        peer = flip(me, d)
        return pltpu.make_async_remote_copy(
            src_ref=store_hbm.at[pl.ds(pl.multiple_of(peer * piece, piece), piece)],
            dst_ref=kv.at[own_rows],
            send_sem=send_sem.at[d],
            recv_sem=recv_sem.at[d],
            device_id=(group, peer),
            device_id_type=MESH,
        )

    def pay_copy(d):
        peer = flip(me, d)
        return pltpu.make_async_remote_copy(
            src_ref=payload.at[peer],
            dst_ref=rows_ref.at[me],
            send_sem=pay_send_sem.at[d],
            recv_sem=pay_recv_sem.at[d],
            device_id=(group, peer),
            device_id_type=MESH,
        )

    order = chunk_order()
    for k in order:
        for d in range(k * peers_per_chunk, (k + 1) * peers_per_chunk):
            if d:
                piece_copy(d).start()

    slot_ids = lax.broadcasted_iota(jnp.int32, (pages, recomp), 0)
    page_of = lax.div(pos_row[...], page_len)
    lane_of = lax.rem(pos_row[...], page_len)
    slot_of = jnp.sum(
        jnp.where(slot_ids == page_of, table_col[...], 0), axis=0, keepdims=True
    )
    hit = slot_ids == slot_of
    lane = page_len + jnp.sum(
        jnp.where(hit, lane_of - page_len, 0).astype(jnp.float32), axis=1, keepdims=True
    )
    fresh_copy.wait()
    by_slot = jnp.dot(
        hit.astype(jnp.bfloat16), fresh[...], preferred_element_type=jnp.float32
    )
    lane = jnp.broadcast_to(lane, (pages, LANES))
    for p in range(n):
        part = slice(p * per_peer, (p + 1) * per_peer)
        payload[p, :, :width] = by_slot[part].astype(jnp.bfloat16)
        payload[p, :, width:] = lane[part].astype(jnp.bfloat16)
    own_pay = pltpu.make_async_copy(payload.at[me], rows_ref.at[me], local_sem.at[3])
    own_pay.start()
    for d in range(1, n):
        pay_copy(d).start()

    def positions(k, carry):
        start = pl.multiple_of(k * chunk, chunk)
        token = start + lax.broadcasted_iota(jnp.int32, (pages, chunk), 1)
        page = lax.broadcasted_iota(jnp.int32, (pages, chunk), 0)
        place = jnp.sum(
            jnp.where(table_col[...] == lax.div(token, page_len), page, 0),
            axis=0,
            keepdims=True,
        )
        place = place * page_len + lax.rem(token[:1], page_len)
        stale = jnp.max(
            jnp.where(place == pos_col[...], 1, 0), axis=0, keepdims=True
        )
        key_pos[:, pl.ds(start, chunk)] = jnp.where(stale > 0, 2**30, place)
        return carry

    lax.fori_loop(0, CHUNKS, positions, 0)

    q_copy.wait()
    for h in range(HQ):
        g, i = h // GROUP, h % GROUP
        q_heads[g, i * recomp : (i + 1) * recomp, :] = q_in[:, h * HD : (h + 1) * HD]

    def scores_of(g, keys, block_bias):
        raw = lax.dot_general(
            q_heads[g], keys, (((1,), (1,)), ((), ())), preferred_element_type=jnp.float32
        )
        cols = keys.shape[0]
        shaped = raw.reshape(GROUP, recomp, cols) * scale + block_bias[None]
        return shaped.reshape(q_rows, cols)

    def lane_sums(weights):
        total = weights[:, :LANES]
        for c in range(LANES, weights.shape[1], LANES):
            total = total + weights[:, c : c + LANES]
        return total

    bias_fresh = jnp.where(pos_row[...] <= pos_col[...], 0.0, NEG)

    for g in range(KVH):
        keys = fresh[:, g * HD : (g + 1) * HD]
        values = fresh[:, (KVH + g) * HD : (KVH + g + 1) * HD]
        s = scores_of(g, keys, bias_fresh)
        m = jnp.max(s, axis=1, keepdims=True)
        w = jnp.exp2(s - m)
        row_max[g] = jnp.broadcast_to(m, (q_rows, LANES))
        row_sum[g] = lane_sums(w)
        acc[g] = jnp.dot(
            w.astype(jnp.bfloat16), values, preferred_element_type=jnp.float32
        )

    for k in order:
        for d in range(k * peers_per_chunk, (k + 1) * peers_per_chunk):
            if d:
                piece_copy(d).wait_recv()
            else:
                own_copy.wait()
        first = flip(lax.div(me, peers_per_chunk), k) * chunk
        rows = pl.ds(pl.multiple_of(first, chunk), chunk)
        bias[...] = jnp.where(key_pos[:, rows] <= pos_col[...], 0.0, NEG)

        def one_group(g, carry):
            keys = kv[rows, pl.ds(pl.multiple_of(g * HD, HD), HD)]
            values = kv[rows, pl.ds(pl.multiple_of((KVH + g) * HD, HD), HD)]
            s = scores_of(g, keys, bias[...])
            old = row_max[g]
            new = jnp.maximum(old, jnp.max(s, axis=1, keepdims=True))
            shrink = jnp.exp2(old - new)
            w = jnp.exp2(s - new[:, :1])
            row_max[g] = new
            row_sum[g] = row_sum[g] * shrink + lane_sums(w)
            acc[g] = acc[g] * shrink + jnp.dot(
                w.astype(jnp.bfloat16), values, preferred_element_type=jnp.float32
            )
            return carry

        lax.fori_loop(0, KVH, one_group, 0)

    for h in range(HQ):
        g, i = h // GROUP, h % GROUP
        part = slice(i * recomp, (i + 1) * recomp)
        total = jnp.sum(row_sum[g, part, :], axis=1, keepdims=True)
        out_ref[:, h * HD : (h + 1) * HD] = (acc[g, part, :] / total).astype(out_ref.dtype)

    own_pay.wait()
    for d in range(1, n):
        piece_copy(d).wait_send()
        pay_copy(d).wait()


def body(n, page_store, page_table, recomp_pos, queries, fresh_kv):
    pages, page_len, width = page_store.shape
    tokens = pages * page_len
    recomp = recomp_pos.shape[1]
    per_peer = pages // n
    q_rows = GROUP * recomp
    vmem = pl.BlockSpec(memory_space=pltpu.VMEM)
    anywhere = pl.BlockSpec(memory_space=pl.ANY)
    attended, rows = pl.pallas_call(
        functools.partial(kernel, n),
        out_shape=(
            jax.ShapeDtypeStruct((recomp, HQ * HD), jnp.bfloat16),
            jax.ShapeDtypeStruct((n, per_peer, width + LANES), jnp.bfloat16),
        ),
        in_specs=[vmem, vmem, vmem, anywhere, anywhere, anywhere],
        out_specs=(vmem, anywhere),
        scratch_shapes=[
            pltpu.VMEM((tokens, width), jnp.bfloat16),
            pltpu.VMEM((recomp, HQ * HD), jnp.bfloat16),
            pltpu.VMEM((recomp, width), jnp.bfloat16),
            pltpu.VMEM((KVH, q_rows, HD), jnp.bfloat16),
            pltpu.VMEM((1, tokens), jnp.int32),
            pltpu.VMEM((recomp, tokens // CHUNKS), jnp.float32),
            pltpu.VMEM((KVH, q_rows, LANES), jnp.float32),
            pltpu.VMEM((KVH, q_rows, LANES), jnp.float32),
            pltpu.VMEM((KVH, q_rows, HD), jnp.float32),
            pltpu.VMEM((n, per_peer, width + LANES), jnp.bfloat16),
            pltpu.SemaphoreType.DMA((n,)),
            pltpu.SemaphoreType.DMA((n,)),
            pltpu.SemaphoreType.DMA((n,)),
            pltpu.SemaphoreType.DMA((n,)),
            pltpu.SemaphoreType.DMA((4,)),
        ],
        compiler_params=pltpu.CompilerParams(
            collective_id=0, has_side_effects=True, vmem_limit_bytes=48 * 2**20
        ),
        name="blend_attend",
    )(
        page_table.reshape(pages, 1),
        recomp_pos,
        recomp_pos.reshape(recomp, 1),
        page_store.reshape(tokens, width),
        queries[0],
        fresh_kv[0],
    )
    paged = page_store.reshape(n, per_peer, page_len, width)
    lane = rows[:, :, width:width + 1].astype(jnp.int32)[:, :, :, None]
    here = lane == jnp.arange(page_len, dtype=jnp.int32)[None, None, :, None]
    new_store = jnp.where(here, rows[:, :, None, :width], paged)
    return (new_store.reshape(pages, page_len, width), attended[None])


def solution(mesh):
    return jax.shard_map(
        functools.partial(body, mesh.shape["cache"]),
        mesh=mesh,
        in_specs=(
            P(("groups", "cache"), None, None),
            P(("groups", "cache"), None),
            P(("groups", "cache"), None),
            P(("groups", "cache"), None, None),
            P(("groups", "cache"), None, None),
        ),
        out_specs=(P(("groups", "cache"), None, None), P(("groups", "cache"), None, None)),
        check_vma=False,
    )
```

```python
import functools
import math

import jax
import jax.numpy as jnp
from jax import lax
from jax.experimental import pallas as pl
from jax.experimental.pallas import tpu as pltpu
from jax.sharding import PartitionSpec as P

HQ = 32
KVH = 4
HD = 128
GROUP = HQ // KVH
CHUNKS = 8
LANES = 128
MESH = pl.DeviceIdType.MESH
NEG = -1e30


def flip(index, bits):
    result = index
    weight = 1
    while weight <= bits:
        if bits & weight:
            own = lax.rem(lax.div(index, weight), 2)
            result = result + weight * (1 - 2 * own)
        weight *= 2
    return result


def column(row):
    size = row.shape[1]
    down = lax.broadcasted_iota(jnp.int32, (size, size), 0)
    along = lax.broadcasted_iota(jnp.int32, (size, size), 1)
    return jnp.sum(jnp.where(down == along, row, 0), axis=1, keepdims=True)


def chunk_order():
    half = CHUNKS // 2
    order = []
    for k in range(half):
        order += [k, half + k]
    return order


def kernel(
    n,
    table_hbm,
    pos_hbm,
    store_hbm,
    queries_hbm,
    fresh_hbm,
    out_ref,
    rows_ref,
    lanes_ref,
    table_row,
    pos_row,
    kv,
    q_in,
    fresh,
    q_heads,
    key_pos,
    bias,
    row_max,
    row_sum,
    acc,
    payload,
    lanes,
    send_sem,
    recv_sem,
    pay_send_sem,
    pay_recv_sem,
    lane_send_sem,
    lane_recv_sem,
    local_sem,
):
    me = lax.axis_index("cache")
    group = lax.axis_index("groups")
    tokens, width = kv.shape
    pages = table_row.shape[1]
    page_len = tokens // pages
    per_peer = pages // n
    piece = tokens // n
    chunk = tokens // CHUNKS
    peers_per_chunk = n // CHUNKS
    recomp = pos_row.shape[1]
    q_rows = GROUP * recomp
    scale = math.log2(math.e) / math.sqrt(HD)

    barrier = pltpu.get_barrier_semaphore()
    for d in range(1, n):
        pl.semaphore_signal(
            barrier, inc=1, device_id=(group, flip(me, d)), device_id_type=MESH
        )
    q_copy = pltpu.make_async_copy(queries_hbm, q_in, local_sem.at[0])
    fresh_copy = pltpu.make_async_copy(fresh_hbm, fresh, local_sem.at[1])
    own_rows = pl.ds(pl.multiple_of(me * piece, piece), piece)
    own_copy = pltpu.make_async_copy(store_hbm.at[own_rows], kv.at[own_rows], local_sem.at[2])
    table_copy = pltpu.make_async_copy(table_hbm, table_row, local_sem.at[4])
    pos_copy = pltpu.make_async_copy(pos_hbm, pos_row, local_sem.at[5])
    table_copy.start()
    pos_copy.start()
    fresh_copy.start()
    q_copy.start()
    own_copy.start()
    pl.semaphore_wait(barrier, n - 1)

    def piece_copy(d):
        peer = flip(me, d)
        return pltpu.make_async_remote_copy(
            src_ref=store_hbm.at[pl.ds(pl.multiple_of(peer * piece, piece), piece)],
            dst_ref=kv.at[own_rows],
            send_sem=send_sem.at[d],
            recv_sem=recv_sem.at[d],
            device_id=(group, peer),
            device_id_type=MESH,
        )

    def pay_copy(d):
        peer = flip(me, d)
        return pltpu.make_async_remote_copy(
            src_ref=payload.at[peer],
            dst_ref=rows_ref.at[me],
            send_sem=pay_send_sem.at[d],
            recv_sem=pay_recv_sem.at[d],
            device_id=(group, peer),
            device_id_type=MESH,
        )

    def lane_copy(d):
        return pltpu.make_async_remote_copy(
            src_ref=lanes,
            dst_ref=lanes_ref.at[me],
            send_sem=lane_send_sem.at[d],
            recv_sem=lane_recv_sem.at[d],
            device_id=(group, flip(me, d)),
            device_id_type=MESH,
        )

    order = chunk_order()
    for k in order:
        for d in range(k * peers_per_chunk, (k + 1) * peers_per_chunk):
            if d:
                piece_copy(d).start()

    table_copy.wait()
    pos_copy.wait()
    table_col = column(table_row[...])
    pos_col = column(pos_row[...])

    slot_ids = lax.broadcasted_iota(jnp.int32, (pages, recomp), 0)
    page_of = lax.div(pos_row[...], page_len)
    slot_of = jnp.sum(
        jnp.where(slot_ids == page_of, table_col, 0), axis=0, keepdims=True
    )
    hit = slot_ids == slot_of
    slots = lax.broadcasted_iota(jnp.int32, (recomp, pages), 1)
    replaced = jnp.where(
        slots == column(slot_of), lax.rem(pos_col, page_len) - page_len, 0
    )
    lanes[...] = page_len + jnp.sum(replaced, axis=0, keepdims=True)
    own_lanes = pltpu.make_async_copy(lanes, lanes_ref.at[me], local_sem.at[6])
    own_lanes.start()
    for d in range(1, n):
        lane_copy(d).start()
    fresh_copy.wait()
    by_slot = jnp.dot(
        hit.astype(jnp.bfloat16), fresh[...], preferred_element_type=jnp.float32
    )
    for p in range(n):
        part = slice(p * per_peer, (p + 1) * per_peer)
        payload[p] = by_slot[part].astype(jnp.bfloat16)
    own_pay = pltpu.make_async_copy(payload.at[me], rows_ref.at[me], local_sem.at[3])
    own_pay.start()
    for d in range(1, n):
        pay_copy(d).start()

    def positions(k, carry):
        start = pl.multiple_of(k * chunk, chunk)
        token = start + lax.broadcasted_iota(jnp.int32, (pages, chunk), 1)
        page = lax.broadcasted_iota(jnp.int32, (pages, chunk), 0)
        place = jnp.sum(
            jnp.where(table_col == lax.div(token, page_len), page, 0),
            axis=0,
            keepdims=True,
        )
        place = place * page_len + lax.rem(token[:1], page_len)
        stale = jnp.max(
            jnp.where(place == pos_col, 1, 0), axis=0, keepdims=True
        )
        key_pos[:, pl.ds(start, chunk)] = jnp.where(stale > 0, 2**30, place)
        return carry

    lax.fori_loop(0, CHUNKS, positions, 0)

    q_copy.wait()
    for h in range(HQ):
        g, i = h // GROUP, h % GROUP
        q_heads[g, i * recomp : (i + 1) * recomp, :] = q_in[:, h * HD : (h + 1) * HD]

    def scores_of(g, keys, block_bias):
        raw = lax.dot_general(
            q_heads[g], keys, (((1,), (1,)), ((), ())), preferred_element_type=jnp.float32
        )
        cols = keys.shape[0]
        shaped = raw.reshape(GROUP, recomp, cols) * scale + block_bias[None]
        return shaped.reshape(q_rows, cols)

    def lane_sums(weights):
        total = weights[:, :LANES]
        for c in range(LANES, weights.shape[1], LANES):
            total = total + weights[:, c : c + LANES]
        return total

    bias_fresh = jnp.where(pos_row[...] <= pos_col, 0.0, NEG)

    for g in range(KVH):
        keys = fresh[:, g * HD : (g + 1) * HD]
        values = fresh[:, (KVH + g) * HD : (KVH + g + 1) * HD]
        s = scores_of(g, keys, bias_fresh)
        m = jnp.max(s, axis=1, keepdims=True)
        w = jnp.exp2(s - m)
        row_max[g] = jnp.broadcast_to(m, (q_rows, LANES))
        row_sum[g] = lane_sums(w)
        acc[g] = jnp.dot(
            w.astype(jnp.bfloat16), values, preferred_element_type=jnp.float32
        )

    for k in order:
        for d in range(k * peers_per_chunk, (k + 1) * peers_per_chunk):
            if d:
                piece_copy(d).wait_recv()
            else:
                own_copy.wait()
        first = flip(lax.div(me, peers_per_chunk), k) * chunk
        rows = pl.ds(pl.multiple_of(first, chunk), chunk)
        bias[...] = jnp.where(key_pos[:, rows] <= pos_col, 0.0, NEG)

        def one_group(g, carry):
            keys = kv[rows, pl.ds(pl.multiple_of(g * HD, HD), HD)]
            values = kv[rows, pl.ds(pl.multiple_of((KVH + g) * HD, HD), HD)]
            s = scores_of(g, keys, bias[...])
            old = row_max[g]
            new = jnp.maximum(old, jnp.max(s, axis=1, keepdims=True))
            shrink = jnp.exp2(old - new)
            w = jnp.exp2(s - new[:, :1])
            row_max[g] = new
            row_sum[g] = row_sum[g] * shrink + lane_sums(w)
            acc[g] = acc[g] * shrink + jnp.dot(
                w.astype(jnp.bfloat16), values, preferred_element_type=jnp.float32
            )
            return carry

        lax.fori_loop(0, KVH, one_group, 0)

    for h in range(HQ):
        g, i = h // GROUP, h % GROUP
        part = slice(i * recomp, (i + 1) * recomp)
        total = jnp.sum(row_sum[g, part, :], axis=1, keepdims=True)
        out_ref[:, h * HD : (h + 1) * HD] = (acc[g, part, :] / total).astype(out_ref.dtype)

    own_lanes.wait()
    own_pay.wait()
    for d in range(1, n):
        piece_copy(d).wait_send()
        lane_copy(d).wait()
        pay_copy(d).wait()


def body(n, page_store, page_table, recomp_pos, queries, fresh_kv):
    pages, page_len, width = page_store.shape
    tokens = pages * page_len
    recomp = recomp_pos.shape[1]
    per_peer = pages // n
    q_rows = GROUP * recomp
    vmem = pl.BlockSpec(memory_space=pltpu.VMEM)
    hbm = pl.BlockSpec(memory_space=pltpu.HBM)
    attended, rows, lanes = pl.pallas_call(
        functools.partial(kernel, n),
        out_shape=(
            jax.ShapeDtypeStruct((recomp, HQ * HD), jnp.bfloat16),
            jax.ShapeDtypeStruct((n, per_peer, width), jnp.bfloat16),
            jax.ShapeDtypeStruct((n, 1, pages), jnp.int32),
        ),
        in_specs=[hbm] * 5,
        out_specs=(vmem, hbm, hbm),
        scratch_shapes=[
            pltpu.VMEM((1, pages), jnp.int32),
            pltpu.VMEM((1, recomp), jnp.int32),
            pltpu.VMEM((tokens, width), jnp.bfloat16),
            pltpu.VMEM((recomp, HQ * HD), jnp.bfloat16),
            pltpu.VMEM((recomp, width), jnp.bfloat16),
            pltpu.VMEM((KVH, q_rows, HD), jnp.bfloat16),
            pltpu.VMEM((1, tokens), jnp.int32),
            pltpu.VMEM((recomp, tokens // CHUNKS), jnp.float32),
            pltpu.VMEM((KVH, q_rows, LANES), jnp.float32),
            pltpu.VMEM((KVH, q_rows, LANES), jnp.float32),
            pltpu.VMEM((KVH, q_rows, HD), jnp.float32),
            pltpu.VMEM((n, per_peer, width), jnp.bfloat16),
            pltpu.VMEM((1, pages), jnp.int32),
            pltpu.SemaphoreType.DMA((n,)),
            pltpu.SemaphoreType.DMA((n,)),
            pltpu.SemaphoreType.DMA((n,)),
            pltpu.SemaphoreType.DMA((n,)),
            pltpu.SemaphoreType.DMA((n,)),
            pltpu.SemaphoreType.DMA((n,)),
            pltpu.SemaphoreType.DMA((7,)),
        ],
        compiler_params=pltpu.CompilerParams(
            collective_id=0, has_side_effects=True, vmem_limit_bytes=62 * 2**20
        ),
        name="blend_attend",
    )(
        page_table,
        recomp_pos,
        page_store.reshape(tokens, width),
        queries[0],
        fresh_kv[0],
    )
    paged = page_store.reshape(n, per_peer, page_len, width)
    first = lax.axis_index("cache") * per_peer
    lane = lax.dynamic_slice_in_dim(lanes[:, 0], first, per_peer, 1)[:, :, None, None]
    here = lane == jnp.arange(page_len, dtype=jnp.int32)[None, None, :, None]
    new_store = jnp.where(here, rows[:, :, None, :], paged)
    return (new_store.reshape(pages, page_len, width), attended[None])


def solution(mesh):
    return jax.shard_map(
        functools.partial(body, mesh.shape["cache"]),
        mesh=mesh,
        in_specs=(
            P(("groups", "cache"), None, None),
            P(("groups", "cache"), None),
            P(("groups", "cache"), None),
            P(("groups", "cache"), None, None),
            P(("groups", "cache"), None, None),
        ),
        out_specs=(P(("groups", "cache"), None, None), P(("groups", "cache"), None, None)),
        check_vma=False,
    )
```

```python
import functools
import math

import jax
import jax.numpy as jnp
from jax import lax
from jax.experimental import pallas as pl
from jax.experimental.pallas import tpu as pltpu
from jax.sharding import PartitionSpec as P

HQ = 32
KVH = 4
HD = 128
GROUP = HQ // KVH
CHUNKS = 8
LANES = 128
MESH = pl.DeviceIdType.MESH
NEG = -1e30


def flip(index, bits):
    result = index
    weight = 1
    while weight <= bits:
        if bits & weight:
            own = lax.rem(lax.div(index, weight), 2)
            result = result + weight * (1 - 2 * own)
        weight *= 2
    return result


def column(row):
    size = row.shape[1]
    down = lax.broadcasted_iota(jnp.int32, (size, size), 0)
    along = lax.broadcasted_iota(jnp.int32, (size, size), 1)
    return jnp.sum(jnp.where(down == along, row, 0), axis=1, keepdims=True)


def chunk_order():
    return list(range(CHUNKS))


def kernel(
    n,
    table_hbm,
    pos_hbm,
    store_hbm,
    queries_hbm,
    fresh_hbm,
    out_ref,
    rows_ref,
    lanes_ref,
    table_row,
    pos_row,
    kv,
    q_in,
    fresh,
    q_heads,
    key_pos,
    bias,
    row_max,
    row_sum,
    acc,
    payload,
    lanes,
    send_sem,
    recv_sem,
    pay_send_sem,
    pay_recv_sem,
    lane_send_sem,
    lane_recv_sem,
    local_sem,
):
    me = lax.axis_index("cache")
    group = lax.axis_index("groups")
    tokens, width = kv.shape
    pages = table_row.shape[1]
    page_len = tokens // pages
    per_peer = pages // n
    piece = tokens // n
    chunk = tokens // CHUNKS
    peers_per_chunk = n // CHUNKS
    recomp = pos_row.shape[1]
    q_rows = GROUP * recomp
    scale = math.log2(math.e) / math.sqrt(HD)

    barrier = pltpu.get_barrier_semaphore()
    for d in range(1, n):
        pl.semaphore_signal(
            barrier, inc=1, device_id=(group, flip(me, d)), device_id_type=MESH
        )
    q_copy = pltpu.make_async_copy(queries_hbm, q_in, local_sem.at[0])
    fresh_copy = pltpu.make_async_copy(fresh_hbm, fresh, local_sem.at[1])
    own_rows = pl.ds(pl.multiple_of(me * piece, piece), piece)
    own_copy = pltpu.make_async_copy(store_hbm.at[own_rows], kv.at[own_rows], local_sem.at[2])
    table_copy = pltpu.make_async_copy(table_hbm, table_row, local_sem.at[4])
    pos_copy = pltpu.make_async_copy(pos_hbm, pos_row, local_sem.at[5])
    table_copy.start()
    pos_copy.start()
    fresh_copy.start()
    q_copy.start()
    own_copy.start()
    pl.semaphore_wait(barrier, n - 1)

    def piece_copy(d):
        peer = flip(me, d)
        return pltpu.make_async_remote_copy(
            src_ref=store_hbm.at[pl.ds(pl.multiple_of(peer * piece, piece), piece)],
            dst_ref=kv.at[own_rows],
            send_sem=send_sem.at[d],
            recv_sem=recv_sem.at[d],
            device_id=(group, peer),
            device_id_type=MESH,
        )

    def pay_copy(d):
        peer = flip(me, d)
        return pltpu.make_async_remote_copy(
            src_ref=payload.at[peer],
            dst_ref=rows_ref.at[me],
            send_sem=pay_send_sem.at[d],
            recv_sem=pay_recv_sem.at[d],
            device_id=(group, peer),
            device_id_type=MESH,
        )

    def lane_copy(d):
        return pltpu.make_async_remote_copy(
            src_ref=lanes,
            dst_ref=lanes_ref.at[me],
            send_sem=lane_send_sem.at[d],
            recv_sem=lane_recv_sem.at[d],
            device_id=(group, flip(me, d)),
            device_id_type=MESH,
        )

    order = chunk_order()
    for k in order:
        for d in range(k * peers_per_chunk, (k + 1) * peers_per_chunk):
            if d:
                piece_copy(d).start()

    table_copy.wait()
    pos_copy.wait()
    table_col = column(table_row[...])
    pos_col = column(pos_row[...])

    slot_ids = lax.broadcasted_iota(jnp.int32, (pages, recomp), 0)
    page_of = lax.div(pos_row[...], page_len)
    slot_of = jnp.sum(
        jnp.where(slot_ids == page_of, table_col, 0), axis=0, keepdims=True
    )
    hit = slot_ids == slot_of
    slots = lax.broadcasted_iota(jnp.int32, (recomp, pages), 1)
    replaced = jnp.where(
        slots == column(slot_of), lax.rem(pos_col, page_len) - page_len, 0
    )
    lanes[...] = page_len + jnp.sum(replaced, axis=0, keepdims=True)
    own_lanes = pltpu.make_async_copy(lanes, lanes_ref.at[me], local_sem.at[6])
    own_lanes.start()
    for d in range(1, n):
        lane_copy(d).start()
    fresh_copy.wait()
    by_slot = jnp.dot(
        hit.astype(jnp.bfloat16), fresh[...], preferred_element_type=jnp.float32
    )
    for p in range(n):
        part = slice(p * per_peer, (p + 1) * per_peer)
        payload[p] = by_slot[part].astype(jnp.bfloat16)
    own_pay = pltpu.make_async_copy(payload.at[me], rows_ref.at[me], local_sem.at[3])
    own_pay.start()
    for d in range(1, n):
        pay_copy(d).start()

    def positions(k, carry):
        start = pl.multiple_of(k * chunk, chunk)
        token = start + lax.broadcasted_iota(jnp.int32, (pages, chunk), 1)
        page = lax.broadcasted_iota(jnp.int32, (pages, chunk), 0)
        place = jnp.sum(
            jnp.where(table_col == lax.div(token, page_len), page, 0),
            axis=0,
            keepdims=True,
        )
        place = place * page_len + lax.rem(token[:1], page_len)
        stale = jnp.max(
            jnp.where(place == pos_col, 1, 0), axis=0, keepdims=True
        )
        key_pos[:, pl.ds(start, chunk)] = jnp.where(stale > 0, 2**30, place)
        return carry

    lax.fori_loop(0, CHUNKS, positions, 0)

    q_copy.wait()
    for h in range(HQ):
        g, i = h // GROUP, h % GROUP
        q_heads[g, i * recomp : (i + 1) * recomp, :] = q_in[:, h * HD : (h + 1) * HD]

    def scores_of(g, keys, block_bias):
        raw = lax.dot_general(
            q_heads[g], keys, (((1,), (1,)), ((), ())), preferred_element_type=jnp.float32
        )
        cols = keys.shape[0]
        shaped = raw.reshape(GROUP, recomp, cols) * scale + block_bias[None]
        return shaped.reshape(q_rows, cols)

    def lane_sums(weights):
        total = weights[:, :LANES]
        for c in range(LANES, weights.shape[1], LANES):
            total = total + weights[:, c : c + LANES]
        return total

    bias_fresh = jnp.where(pos_row[...] <= pos_col, 0.0, NEG)

    for g in range(KVH):
        keys = fresh[:, g * HD : (g + 1) * HD]
        values = fresh[:, (KVH + g) * HD : (KVH + g + 1) * HD]
        s = scores_of(g, keys, bias_fresh)
        m = jnp.max(s, axis=1, keepdims=True)
        w = jnp.exp2(s - m)
        row_max[g] = jnp.broadcast_to(m, (q_rows, LANES))
        row_sum[g] = lane_sums(w)
        acc[g] = jnp.dot(
            w.astype(jnp.bfloat16), values, preferred_element_type=jnp.float32
        )

    for k in order:
        for d in range(k * peers_per_chunk, (k + 1) * peers_per_chunk):
            if d:
                piece_copy(d).wait_recv()
            else:
                own_copy.wait()
        first = flip(lax.div(me, peers_per_chunk), k) * chunk
        rows = pl.ds(pl.multiple_of(first, chunk), chunk)
        bias[...] = jnp.where(key_pos[:, rows] <= pos_col, 0.0, NEG)

        def one_group(g, carry):
            keys = kv[rows, pl.ds(pl.multiple_of(g * HD, HD), HD)]
            values = kv[rows, pl.ds(pl.multiple_of((KVH + g) * HD, HD), HD)]
            s = scores_of(g, keys, bias[...])
            old = row_max[g]
            new = jnp.maximum(old, jnp.max(s, axis=1, keepdims=True))
            shrink = jnp.exp2(old - new)
            w = jnp.exp2(s - new[:, :1])
            row_max[g] = new
            row_sum[g] = row_sum[g] * shrink + lane_sums(w)
            acc[g] = acc[g] * shrink + jnp.dot(
                w.astype(jnp.bfloat16), values, preferred_element_type=jnp.float32
            )
            return carry

        lax.fori_loop(0, KVH, one_group, 0)

    for h in range(HQ):
        g, i = h // GROUP, h % GROUP
        part = slice(i * recomp, (i + 1) * recomp)
        total = jnp.sum(row_sum[g, part, :], axis=1, keepdims=True)
        out_ref[:, h * HD : (h + 1) * HD] = (acc[g, part, :] / total).astype(out_ref.dtype)

    own_lanes.wait()
    own_pay.wait()
    for d in range(1, n):
        piece_copy(d).wait_send()
        lane_copy(d).wait()
        pay_copy(d).wait()


def body(n, page_store, page_table, recomp_pos, queries, fresh_kv):
    pages, page_len, width = page_store.shape
    tokens = pages * page_len
    recomp = recomp_pos.shape[1]
    per_peer = pages // n
    q_rows = GROUP * recomp
    vmem = pl.BlockSpec(memory_space=pltpu.VMEM)
    hbm = pl.BlockSpec(memory_space=pltpu.HBM)
    attended, rows, lanes = pl.pallas_call(
        functools.partial(kernel, n),
        out_shape=(
            jax.ShapeDtypeStruct((recomp, HQ * HD), jnp.bfloat16),
            jax.ShapeDtypeStruct((n, per_peer, width), jnp.bfloat16),
            jax.ShapeDtypeStruct((n, 1, pages), jnp.int32),
        ),
        in_specs=[hbm] * 5,
        out_specs=(vmem, hbm, hbm),
        scratch_shapes=[
            pltpu.VMEM((1, pages), jnp.int32),
            pltpu.VMEM((1, recomp), jnp.int32),
            pltpu.VMEM((tokens, width), jnp.bfloat16),
            pltpu.VMEM((recomp, HQ * HD), jnp.bfloat16),
            pltpu.VMEM((recomp, width), jnp.bfloat16),
            pltpu.VMEM((KVH, q_rows, HD), jnp.bfloat16),
            pltpu.VMEM((1, tokens), jnp.int32),
            pltpu.VMEM((recomp, tokens // CHUNKS), jnp.float32),
            pltpu.VMEM((KVH, q_rows, LANES), jnp.float32),
            pltpu.VMEM((KVH, q_rows, LANES), jnp.float32),
            pltpu.VMEM((KVH, q_rows, HD), jnp.float32),
            pltpu.VMEM((n, per_peer, width), jnp.bfloat16),
            pltpu.VMEM((1, pages), jnp.int32),
            pltpu.SemaphoreType.DMA((n,)),
            pltpu.SemaphoreType.DMA((n,)),
            pltpu.SemaphoreType.DMA((n,)),
            pltpu.SemaphoreType.DMA((n,)),
            pltpu.SemaphoreType.DMA((n,)),
            pltpu.SemaphoreType.DMA((n,)),
            pltpu.SemaphoreType.DMA((7,)),
        ],
        compiler_params=pltpu.CompilerParams(
            collective_id=0, has_side_effects=True, vmem_limit_bytes=62 * 2**20
        ),
        name="blend_attend",
    )(
        page_table,
        recomp_pos,
        page_store.reshape(tokens, width),
        queries[0],
        fresh_kv[0],
    )
    paged = page_store.reshape(n, per_peer, page_len, width)
    first = lax.axis_index("cache") * per_peer
    lane = lax.dynamic_slice_in_dim(lanes[:, 0], first, per_peer, 1)[:, :, None, None]
    here = lane == jnp.arange(page_len, dtype=jnp.int32)[None, None, :, None]
    new_store = jnp.where(here, rows[:, :, None, :], paged)
    return (new_store.reshape(pages, page_len, width), attended[None])


def solution(mesh):
    return jax.shard_map(
        functools.partial(body, mesh.shape["cache"]),
        mesh=mesh,
        in_specs=(
            P(("groups", "cache"), None, None),
            P(("groups", "cache"), None),
            P(("groups", "cache"), None),
            P(("groups", "cache"), None, None),
            P(("groups", "cache"), None, None),
        ),
        out_specs=(P(("groups", "cache"), None, None), P(("groups", "cache"), None, None)),
        check_vma=False,
    )
```
